32 devices in a mesh: group: 2 (over x), seq: 16 (over z, y, core).
Axes of the slice: x: 2, y: 2, z: 4, core: 2. Of those that a mesh axis runs over, the one named last changes fastest.
Arguments:
- queries: bfloat16 [8192, 2048], P(('group', 'seq')), parts along dimension 0, may hold values from -9 to 9
- keys: bfloat16 [8192, 2048], P(('group', 'seq')), parts along dimension 0, may hold values from -9 to 9
- values: bfloat16 [8192, 2048], P(('group', 'seq')), parts along dimension 0, may hold values from -6 to 6
- query_dir: bfloat16 [8192, 2048], P(('group', 'seq')), parts along dimension 0, may hold values from -6 to 6
- key_dir: bfloat16 [8192, 2048], P(('group', 'seq')), parts along dimension 0, may hold values from -6 to 6
- value_dir: bfloat16 [8192, 2048], P(('group', 'seq')), parts along dimension 0, may hold values from -6 to 6
- window_width: int32 [32], P('group'), parts along dimension 0, may hold values from 0 to 2, as said below
- global_blocks: int32 [32, 2], P('group'), parts along dimension 0, may hold values from 0 to 63
- random_blocks: int32 [32, 64, 2], P('group'), parts along dimension 0, may hold values from 0 to 63
Outputs:
- query_gn: bfloat16 [8192, 2048], P(('group', 'seq')), parts along dimension 0
- key_gn: bfloat16 [8192, 2048], P(('group', 'seq')), parts along dimension 0
- value_gn: bfloat16 [8192, 2048], P(('group', 'seq')), parts along dimension 0
The draws below stay inside these ranges and needn't reach their ends.
There are 2 independent parts, one for each index of `group`. The reference program is written for one: setup_inputs(seed, part) draws one part's arguments, and reference() takes and returns one part's arrays. A program takes and returns all parts, laid end to end along the dimension named above; each array names one. Nothing has to cross between parts.
Inputs may be any that keep to these rules, and one draw needn't show every extreme that they name: `window_width`: the values 0 and 2 both occur.
All inputs are finite; a program needn't handle non-finite values.
Results may differ from the reference program's by a relative error of at most 0.013.
Values may be sent and summed in bfloat16 or wider, within the bound.
A program may use at most 128 MiB of HBM per device.

```python
import math
import jax
import jax.numpy as jnp
from jax import lax

HEADS = 16
HDIM = 128
BLOCK = 64
WMAX = 2
NGLOB = 2
NRAND = 2
SEQ_LEN = 4096
NBLK = 64


def draw_queries(key, part):
    key = jax.random.fold_in(key, 3)
    return jnp.clip(jax.random.normal(key, (SEQ_LEN, HEADS * HDIM)), -6.0, 6.0).astype(jnp.bfloat16)


def draw_keys(key, part):
    key = jax.random.fold_in(key, 5)
    return jnp.clip(jax.random.normal(key, (SEQ_LEN, HEADS * HDIM)), -6.0, 6.0).astype(jnp.bfloat16)


def draw_window_width(key, part):
    key = jax.random.fold_in(key, 7)
    return (jax.random.permutation(key, HEADS) % (WMAX + 1)).astype(jnp.int32)


def place_ends(values, stream_key, smallest, high):
    place = [jax.random.randint(jax.random.fold_in(stream_key, axis), (), 0, length) for axis, length in enumerate(values.shape)]
    widest = values.shape.index(max(values.shape))
    neighbour = place[:widest] + [(place[widest] + 1) % values.shape[widest]] + place[widest + 1:]
    return values.at[tuple(place)].set(smallest).at[tuple(neighbour)].set(high)


def shard_levels(key, shape, shards, low, top_value):
    gain, own = 1.0, jax.random.fold_in(key, 6)
    for axis_at, blocks in shards:
        draws = jnp.exp(jax.random.uniform(jax.random.fold_in(own, axis_at), (blocks,), jnp.float32, low / len(shards), top_value / len(shards)))
        gain = gain * jnp.repeat(draws, shape[axis_at] // blocks).reshape([-1 if axis == axis_at else 1 for axis in range(len(shape))])
    return gain


def noise(rng, dims, width, reach, cuts=(), held_as=jnp.bfloat16):
    drawn = jax.random.normal(rng, dims, jnp.float32) * width
    if len(cuts) > 0:
        drawn = shard_levels(rng, dims, cuts, -0.22, 0.18) * drawn
    return jnp.clip(drawn, min=-reach, max=reach).astype(held_as)


def setup_inputs(seed: int = 0, part: int = 0) -> dict:
    key_list = jax.random.split(jax.random.key(seed), 10)
    own_keys = jax.random.split(jax.random.fold_in(key_list[9], part), 10)
    return {
        "queries": draw_queries(jax.random.fold_in(jax.random.fold_in(key_list[9], part), 71), part),
        "keys": draw_keys(jax.random.fold_in(jax.random.fold_in(key_list[9], part), 71), part),
        "values": noise(own_keys[2], (SEQ_LEN, HEADS * HDIM), 1.0, 6.0, ((0, 16),)),
        "query_dir": noise(own_keys[3], (SEQ_LEN, HEADS * HDIM), 1.0, 6.0, ((0, 16),)),
        "key_dir": noise(own_keys[4], (SEQ_LEN, HEADS * HDIM), 1.0, 6.0, ((0, 16),)),
        "value_dir": noise(own_keys[5], (SEQ_LEN, HEADS * HDIM), 1.0, 6.0, ((0, 16),)),
        "window_width": draw_window_width(jax.random.fold_in(jax.random.fold_in(key_list[9], part), 71), part),
        "global_blocks": place_ends(jax.random.randint(own_keys[7], (HEADS, NGLOB), 0, NBLK), jax.random.fold_in(own_keys[7], 1), 0, NBLK - 1).astype(jnp.int32),
        "random_blocks": place_ends(jax.random.randint(own_keys[8], (HEADS, NBLK, NRAND), 0, NBLK), jax.random.fold_in(own_keys[8], 1), 0, NBLK - 1).astype(jnp.int32),
    }


step_blocks = 8
neg_fill = -1e+30

def key_slots(query_ids, head_window, head_globals, head_randoms, block_count, window_reach):
    offsets = jnp.arange(-window_reach, window_reach + 1, dtype=jnp.int32)
    named_ids = query_ids[:, None] + offsets[None, :]
    window_live = (jnp.abs(offsets)[None, :] <= head_window) & (named_ids >= 0) & (named_ids < block_count)
    window_ids = jnp.clip(named_ids, 0, block_count - 1)
    row_count = query_ids.shape[0]
    global_ids = jnp.broadcast_to(head_globals[None, :], (row_count, head_globals.shape[0]))
    slot_ids = jnp.concatenate([window_ids, global_ids.astype(jnp.int32), head_randoms.astype(jnp.int32)], axis=1)
    always_live = jnp.ones((row_count, head_globals.shape[0] + head_randoms.shape[1]), dtype=bool)
    return (slot_ids.astype(jnp.int32), jnp.concatenate([window_live, always_live], axis=1))

def attend(query_block, key_block, value_block, is_live):
    score_scale = 1.0 / math.sqrt(query_block.shape[-1])
    scores = jnp.einsum('gqe,gske->gqsk', query_block, key_block) * score_scale
    scores = jnp.where(is_live[:, None, :, None], scores, neg_fill)
    row_top = lax.stop_gradient(lax.optimization_barrier(jnp.max(scores, axis=(2, 3), keepdims=True)))
    weights_raw = jnp.exp(scores - row_top)
    row_total = lax.optimization_barrier(jnp.sum(weights_raw, axis=(2, 3), keepdims=True))
    return jnp.einsum('gqsk,gske->gqe', weights_raw / row_total, value_block)

def gauss_newton(query_block, key_block, value_block, query_tan, key_tan, value_tan, is_live):

    def forward(query_arg, key_arg, value_arg):
        return attend(query_arg, key_arg, value_arg, is_live)
    primal_out, tangent = jax.jvp(forward, (query_block, key_block, value_block), (query_tan, key_tan, value_tan))
    primal_again, pull_back = jax.vjp(forward, query_block, key_block, value_block)
    return pull_back(tangent)

def gn_head(query_rows, query_dirs, query_ids, key_rows, value_rows, key_dirs, value_dirs, head_window, head_globals, head_randoms, window_reach):
    block_count = key_rows.shape[0]
    float_type = jnp.float32
    step_count = query_rows.shape[0] // step_blocks

    def by_step(array):
        return array.reshape((step_count, step_blocks) + array.shape[1:])

    def one_step(totals, step_item):
        key_acc, value_acc = totals
        query_block, query_tan, step_ids, step_randoms = step_item
        slot_ids, is_live = key_slots(step_ids, head_window, head_globals, step_randoms, block_count, window_reach)
        key_block = key_rows[slot_ids].astype(float_type)
        value_block = value_rows[slot_ids].astype(float_type)
        key_tan = key_dirs[slot_ids].astype(float_type)
        value_tan = value_dirs[slot_ids].astype(float_type)
        query_part, key_part, value_part = gauss_newton(query_block.astype(float_type), key_block, value_block, query_tan.astype(float_type), key_tan, value_tan, is_live)
        key_acc = key_acc.at[slot_ids].add(key_part)
        value_acc = value_acc.at[slot_ids].add(value_part)
        return ((key_acc, value_acc), query_part)
    zero_grads = jnp.zeros(key_rows.shape, float_type)
    (key_grad, value_grad), query_grad = lax.scan(one_step, (zero_grads, zero_grads), (by_step(query_rows), by_step(query_dirs), by_step(query_ids), by_step(head_randoms)))
    return (query_grad.reshape(query_rows.shape), key_grad, value_grad)

def reference(queries, keys, values, query_dir, key_dir, value_dir, window_width, global_blocks, random_blocks):
    block_count = SEQ_LEN // BLOCK

    def by_head(array):
        return array.reshape(block_count, BLOCK, HEADS, HDIM).transpose(2, 0, 1, 3)
    query_ids = jnp.arange(block_count, dtype=jnp.int32)

    def per_head(head_item):
        query_h, qdir_h, key_h, value_h, kdir_h, vdir_h, head_window, head_globals, head_randoms = head_item
        return gn_head(query_h, qdir_h, query_ids, key_h, value_h, kdir_h, vdir_h, head_window, head_globals, head_randoms, WMAX)
    query_grad, key_grad, value_grad = lax.map(per_head, (by_head(queries), by_head(query_dir), by_head(keys), by_head(values), by_head(key_dir), by_head(value_dir), window_width, global_blocks, random_blocks))

    def to_rows(array):
        return array.transpose(1, 2, 0, 3).reshape(SEQ_LEN, HEADS * HDIM).astype(jnp.bfloat16)
    return (to_rows(query_grad), to_rows(key_grad), to_rows(value_grad))
```

```python
import functools
import math

import jax
import jax.numpy as jnp
from jax import lax
from jax.experimental import pallas as pl
from jax.experimental.pallas import tpu as pltpu
from jax.sharding import PartitionSpec as P

BLOCK = 64
WMAX = 2
PAIR = 2 * BLOCK
neg_fill = -1e30
f32 = jnp.float32
bf16 = jnp.bfloat16


def dot(lhs, rhs, lhs_dim, rhs_dim):
    return lax.dot_general(
        lhs, rhs, (((lhs_dim,), (rhs_dim,)), ((), ())), preferred_element_type=f32
    )


def attend_kernel(
    pairs, slots, live, q, dq, k, v, dk, dv, q_out, k_out, v_out, k_acc, v_acc
):
    step = pl.program_id(0)
    head_dim = q.shape[1]
    scale = 1.0 / math.sqrt(head_dim)
    slot_count = 2 * WMAX + 2 + 2 + 4
    keys = slot_count * BLOCK

    @pl.when(step == 0)
    def _():
        k_acc[...] = jnp.zeros_like(k_acc)
        v_acc[...] = jnp.zeros_like(v_acc)

    def gather(ref, starts):
        return jnp.concatenate([ref[pl.ds(start, BLOCK), :] for start in starts], axis=0)

    blank = jnp.zeros((PAIR, head_dim), bf16)
    added = []
    for pair in range(pairs):
        rows = pl.ds(pair * PAIR, PAIR)
        qb, dqb = q[rows, :], dq[rows, :]
        index = step * pairs + pair
        starts = [
            pl.multiple_of(slots[index, s] * BLOCK, BLOCK) for s in range(slot_count)
        ]
        kg, vg = gather(k, starts), gather(v, starts)
        kk = jnp.concatenate([kg, gather(dk, starts)], axis=1)
        vv = jnp.concatenate([vg, gather(dv, starts)], axis=1)
        lhs = jnp.concatenate(
            [jnp.concatenate([qb, blank], axis=1), jnp.concatenate([dqb, qb], axis=1)], axis=0
        )
        both = dot(lhs, kk, 1, 1)
        live_rows = live[pair]
        bias = jnp.concatenate(
            [jnp.broadcast_to(live_rows[h : h + 1, :], (BLOCK, keys)) for h in range(2)], axis=0
        )
        scores = jnp.where(bias > 0.5, both[:PAIR] * scale, neg_fill)
        moved = both[PAIR:] * scale
        top = jnp.max(scores, axis=1, keepdims=True)
        weights = jnp.exp(scores - top)
        weights = weights * (1.0 / jnp.sum(weights, axis=1, keepdims=True))
        mean = jnp.sum(weights * moved, axis=1, keepdims=True)
        weights_dot = weights * (moved - mean)
        wb = weights.astype(bf16)
        out = dot(jnp.concatenate([wb, weights_dot.astype(bf16)], axis=0), vv, 1, 0)
        tangent = (out[:PAIR, head_dim:] + out[PAIR:, :head_dim]).astype(bf16)
        pulled = dot(tangent, vg, 1, 1)
        centre = jnp.sum(weights * pulled, axis=1, keepdims=True)
        ds = (weights * (pulled - centre) * scale).astype(bf16)
        q_out[rows, :] = dot(ds, kg, 1, 0).astype(q_out.dtype)
        rhs = jnp.concatenate(
            [jnp.concatenate([qb, blank], axis=1), jnp.concatenate([blank, tangent], axis=1)],
            axis=0,
        )
        added.append((starts, dot(jnp.concatenate([ds, wb], axis=0), rhs, 0, 0)))
    for starts, part in added:
        for s, start in enumerate(starts):
            rows = pl.ds(start, BLOCK)
            piece = slice(s * BLOCK, (s + 1) * BLOCK)
            k_acc[rows, :] += part[piece, :head_dim]
            v_acc[rows, :] += part[piece, head_dim:]

    @pl.when(step == pl.num_programs(0) - 1)
    def _():
        k_out[...] = k_acc[...].astype(k_out.dtype)
        v_out[...] = v_acc[...].astype(v_out.dtype)


def pair_slots(first_ids, head_window, head_globals, head_randoms, block_count):
    count = first_ids.shape[0]
    offsets = jnp.arange(-WMAX, WMAX + 2, dtype=jnp.int32)
    named = first_ids[:, None] + offsets[None, :]
    inside = (named >= 0) & (named < block_count)
    halves = [
        inside & (jnp.abs(offsets - half)[None, :] <= head_window) for half in range(2)
    ]
    ones = jnp.ones((count, 2), bool)
    none = jnp.zeros((count, 2), bool)
    ids = jnp.concatenate(
        [
            jnp.clip(named, 0, block_count - 1),
            jnp.broadcast_to(head_globals[None, :], (count, 2)),
            head_randoms[first_ids],
            head_randoms[first_ids + 1],
        ],
        axis=1,
    )
    live = jnp.stack(
        [
            jnp.concatenate([halves[0], ones, ones, none], axis=1),
            jnp.concatenate([halves[1], ones, none, ones], axis=1),
        ],
        axis=1,
    )
    return ids, jnp.repeat(live.astype(f32), BLOCK, axis=2)


def head_product(rows, slots, live):
    q, k, v, dq, dk, dv = rows
    query_count, head_dim = q.shape
    tokens = k.shape[0]
    pairs = 2
    while query_count % (pairs * PAIR):
        pairs -= 1
    step_rows = pairs * PAIR
    whole = pl.BlockSpec((tokens, head_dim), lambda i, *_: (0, 0))
    part = pl.BlockSpec((step_rows, head_dim), lambda i, *_: (i, 0))
    like = lambda n: jax.ShapeDtypeStruct((n, head_dim), bf16)
    return pl.pallas_call(
        functools.partial(attend_kernel, pairs),
        grid_spec=pltpu.PrefetchScalarGridSpec(
            num_scalar_prefetch=1,
            grid=(query_count // step_rows,),
            in_specs=[
                pl.BlockSpec((pairs,) + live.shape[1:], lambda i, *_: (i, 0, 0)),
                part,
                part,
                whole,
                whole,
                whole,
                whole,
            ],
            out_specs=[part, whole, whole],
            scratch_shapes=[
                pltpu.VMEM((tokens, head_dim), f32),
                pltpu.VMEM((tokens, head_dim), f32),
            ],
        ),
        out_shape=[like(query_count), like(tokens), like(tokens)],
        compiler_params=pltpu.CompilerParams(
            dimension_semantics=("arbitrary",), vmem_limit_bytes=56 * 1024 * 1024
        ),
    )(slots, live, q, dq, k, v, dk, dv)


def shards(
    queries, keys, values, query_dir, key_dir, value_dir, window_width, global_blocks, random_blocks
):
    devices = lax.axis_size("seq")
    head_count = window_width.shape[0]
    group_size = devices // head_count
    device_index = lax.axis_index("seq")
    head_id = device_index // group_size
    residue = device_index % group_size
    tokens, features = queries.shape
    head_dim = features // head_count
    local_blocks = tokens // BLOCK
    own_blocks = local_blocks // group_size
    own = own_blocks * BLOCK
    block_count = local_blocks * devices

    def swap(array):
        return lax.all_to_all(array, "seq", split_axis=0, concat_axis=0, tiled=True)

    def to_owner(array):
        array = array.reshape(group_size, own, head_count, head_dim).transpose(2, 0, 1, 3)
        return swap(array.reshape(devices * own, head_dim))

    def to_every(array):
        array = array.reshape(tokens, head_count, head_dim).transpose(1, 0, 2)
        array = jnp.broadcast_to(array[:, None], (head_count, group_size, tokens, head_dim))
        return swap(array.reshape(devices * tokens, head_dim))

    rows = [
        to_owner(queries),
        to_every(keys),
        to_every(values),
        to_owner(query_dir),
        to_every(key_dir),
        to_every(value_dir),
    ]
    counter = 2 * jnp.arange(devices * own_blocks // 2, dtype=jnp.int32)
    first_ids = counter // own_blocks * local_blocks + residue * own_blocks + counter % own_blocks
    slots, live = pair_slots(
        first_ids,
        window_width[head_id],
        global_blocks[head_id],
        random_blocks[head_id],
        block_count,
    )
    query_grad, key_grad, value_grad = head_product(rows, slots, live)
    query_gn = (
        swap(query_grad)
        .reshape(head_count, group_size, own, head_dim)
        .transpose(1, 2, 0, 3)
        .reshape(tokens, features)
    )

    def owner_sum(array):
        array = swap(array).reshape(head_count, group_size, tokens, head_dim)
        array = array[:, 0] if group_size == 1 else array.astype(f32).sum(axis=1).astype(bf16)
        return array.transpose(1, 0, 2).reshape(tokens, features)

    return (query_gn, owner_sum(key_grad), owner_sum(value_grad))


def solution(mesh):
    rows = P(("group", "seq"), None)
    placed = (rows,) * 6 + (P("group"), P("group", None), P("group", None, None))
    return jax.shard_map(
        shards, mesh=mesh, in_specs=placed, out_specs=(rows,) * 3, check_vma=False
    )
```

```python
import functools
import math

import jax
import jax.numpy as jnp
from jax import lax
from jax.experimental import pallas as pl
from jax.experimental.pallas import tpu as pltpu
from jax.sharding import PartitionSpec as P

BLOCK = 64
WMAX = 2
PAIR = 2 * BLOCK
SLOTS = 2 * WMAX + 2 + 2 + 4
STRIDE = 7
MESH = pl.DeviceIdType.MESH
neg_fill = -1e30
f32 = jnp.float32
bf16 = jnp.bfloat16


def dot(lhs, rhs, lhs_dim, rhs_dim):
    return lax.dot_general(
        lhs, rhs, (((lhs_dim,), (rhs_dim,)), ((), ())), preferred_element_type=f32
    )


def pair_product(qb, dqb, kg, vg, dkg, dvg, live_rows):
    head_dim = qb.shape[1]
    scale = 1.0 / math.sqrt(head_dim)
    blank = jnp.zeros((PAIR, head_dim), bf16)
    kk = jnp.concatenate([kg, dkg], axis=1)
    vv = jnp.concatenate([vg, dvg], axis=1)
    first = jnp.concatenate([qb, blank], axis=1)
    lhs = jnp.concatenate([first, jnp.concatenate([dqb, qb], axis=1)], axis=0)
    both = dot(lhs, kk, 1, 1)
    bias = jnp.concatenate(
        [jnp.broadcast_to(live_rows[h : h + 1, :], (BLOCK, SLOTS * BLOCK)) for h in range(2)],
        axis=0,
    )
    scores = jnp.where(bias > 0.5, both[:PAIR] * scale, neg_fill)
    moved = both[PAIR:] * scale
    top = jnp.max(scores, axis=1, keepdims=True)
    weights = jnp.exp(scores - top)
    weights = weights * (1.0 / jnp.sum(weights, axis=1, keepdims=True))
    mean = jnp.sum(weights * moved, axis=1, keepdims=True)
    wb = weights.astype(bf16)
    weights_dot = (weights * (moved - mean)).astype(bf16)
    out = dot(jnp.concatenate([wb, weights_dot], axis=0), vv, 1, 0)
    tangent = (out[:PAIR, head_dim:] + out[PAIR:, :head_dim]).astype(bf16)
    pulled = dot(tangent, vg, 1, 1)
    centre = jnp.sum(weights * pulled, axis=1, keepdims=True)
    ds = (weights * (pulled - centre) * scale).astype(bf16)
    query_part = dot(ds, kg, 1, 0).astype(bf16)
    rhs = jnp.concatenate([first, jnp.concatenate([blank, tangent], axis=1)], axis=0)
    return query_part, dot(jnp.concatenate([ds, wb], axis=0), rhs, 0, 0)


def greet(me, devices):
    barrier = pltpu.get_barrier_semaphore()
    for step in range(1, devices):
        pl.semaphore_signal(
            barrier, inc=1, device_id={"seq": lax.rem(me + step, devices)}, device_id_type=MESH
        )
    pl.semaphore_wait(barrier, devices - 1)


def columns(head, head_dim):
    return pl.ds(pl.multiple_of(head * head_dim, head_dim), head_dim)


def rows_at(index, count):
    return pl.ds(pl.multiple_of(index * count, count), count)


def main_kernel(
    devices, group_size,
    slots, live, q, k, v, dq, dk, dv,
    q_gn, window, fixed, drawn,
    q_all, k_all, v_all, dq_all, dk_all, dv_all, q_res,
    send, recv, q_send, q_recv,
):
    me = lax.axis_index("seq")
    local_blocks = k.shape[0]
    tokens = local_blocks * BLOCK
    head_dim = k_all.shape[2]
    own = tokens // group_size
    pairs = own // PAIR
    head, residue = me // group_size, lax.rem(me, group_size)
    kinds = [(k, k_all), (dk, dk_all), (v, v_all), (dv, dv_all), (q, q_all), (dq, dq_all)]
    greet(me, devices)

    def copy(kind, step):
        source, target = kinds[kind]
        to = lax.rem(me + (devices - step * STRIDE % devices), devices)
        if kind < 4:
            part = source.at[:, :, columns(to // group_size, head_dim)]
            spot = target.at[rows_at(me, local_blocks)]
        else:
            part = source.at[
                rows_at(lax.rem(to, group_size), own), columns(to // group_size, head_dim)
            ]
            spot = target.at[rows_at(me, own), :]
        if step == 0:
            return pltpu.make_async_copy(part, spot, recv.at[kind, 0])
        return pltpu.make_async_remote_copy(
            src_ref=part,
            dst_ref=spot,
            send_sem=send.at[kind, step],
            recv_sem=recv.at[kind, step],
            device_id={"seq": to},
            device_id_type=MESH,
        )

    for kind in range(6):
        for step in range(devices):
            copy(kind, step).start()
    window[...] = jnp.zeros_like(window)
    fixed[...] = jnp.zeros_like(fixed)
    for kind in range(4):
        for step in range(devices):
            if step == 0:
                copy(kind, step).wait()
            else:
                copy(kind, step).wait_recv()

    def gather(ref, ids):
        return jnp.concatenate([ref[i] for i in ids], axis=0)

    def back(step, origin):
        part = q_res.at[rows_at(origin, own), :]
        target = q_gn.at[rows_at(residue, own), columns(head, head_dim)]
        return pltpu.make_async_remote_copy(
            src_ref=part,
            dst_ref=target,
            send_sem=q_send.at[step],
            recv_sem=q_recv.at[step],
            device_id={"seq": origin},
            device_id_type=MESH,
        )

    def work(step):
        origin = lax.rem(me + step * STRIDE, devices)
        for pair in range(pairs):
            index = origin * pairs + pair
            rows = rows_at(index, PAIR)
            ids = [slots[index, s] for s in range(SLOTS)]
            query_part, added = pair_product(
                q_all[rows, :], dq_all[rows, :],
                gather(k_all, ids), gather(v_all, ids),
                gather(dk_all, ids), gather(dv_all, ids),
                live[index],
            )
            q_res[rows, :] = query_part
            first = origin * (tokens // BLOCK) + residue * (own // BLOCK) + 2 * pair
            near = (2 * WMAX + 2) * BLOCK
            spot = pl.ds(pl.multiple_of(first * BLOCK, BLOCK), near)
            window[spot, :] += added[:near]
            fixed[...] += added[near : near + PAIR]
            drawn[rows_at(index, 2 * PAIR), :] = added[near + PAIR :].astype(bf16)
        return origin

    own_copy = pltpu.make_async_copy(
        q_res.at[rows_at(me, own), :],
        q_gn.at[rows_at(residue, own), columns(head, head_dim)],
        q_recv.at[0],
    )
    copy(4, 0).wait()
    copy(5, 0).wait()
    work(0)
    own_copy.start()

    def wait_rows(kind, step):
        source, target = kinds[kind]
        pltpu.make_async_remote_copy(
            src_ref=source.at[rows_at(residue, own), columns(head, head_dim)],
            dst_ref=target.at[rows_at(lax.rem(me + step * STRIDE, devices), own), :],
            send_sem=send.at[kind, step],
            recv_sem=recv.at[kind, step],
            device_id={"seq": lax.rem(me + step * STRIDE, devices)},
            device_id_type=MESH,
        ).wait_recv()

    @pl.loop(1, devices)
    def _(step):
        wait_rows(4, step)
        wait_rows(5, step)
        origin = work(step)
        back(step, origin).start()

    for kind in range(6):
        for step in range(1, devices):
            copy(kind, step).wait_send()
    own_copy.wait()
    for step in range(1, devices):
        giver = lax.rem(me + (devices - step * STRIDE % devices), devices)
        pltpu.make_async_remote_copy(
            src_ref=q_res.at[rows_at(giver, own), :],
            dst_ref=q_gn.at[
                rows_at(lax.rem(giver, group_size), own),
                columns(giver // group_size, head_dim),
            ],
            send_sem=q_send.at[step],
            recv_sem=q_recv.at[step],
            device_id={"seq": giver},
            device_id_type=MESH,
        ).wait()


def add_kernel(slots, window, fixed, drawn, k_out, v_out, acc):
    tokens, head_dim = k_out.shape
    acc[...] = window[pl.ds(WMAX * BLOCK, tokens), :]
    for s in range(2):
        rows = rows_at(slots[0, 2 * WMAX + 2 + s], BLOCK)
        acc[rows, :] += fixed[s * BLOCK : (s + 1) * BLOCK, :]

    @pl.loop(0, slots.shape[0])
    def _(index):
        for s in range(4):
            rows = rows_at(slots[index, 2 * WMAX + 4 + s], BLOCK)
            acc[rows, :] += drawn[rows_at(index * 4 + s, BLOCK), :].astype(f32)

    k_out[...] = acc[:, :head_dim].astype(bf16)
    v_out[...] = acc[:, head_dim:].astype(bf16)


def return_kernel(devices, group_size, k, v, k_gn, v_gn, send, recv):
    me = lax.axis_index("seq")
    tokens, head_dim = k.shape[0] // devices, k.shape[1]
    greet(me, devices)

    def copy(kind, step):
        source, target = ((k, k_gn), (v, v_gn))[kind]
        to = lax.rem(me + step * STRIDE, devices)
        part = source.at[rows_at(to, tokens), :]
        spot = target.at[lax.rem(me, group_size), :, columns(me // group_size, head_dim)]
        if step == 0:
            return pltpu.make_async_copy(part, spot, recv.at[kind, 0])
        return pltpu.make_async_remote_copy(
            src_ref=part,
            dst_ref=spot,
            send_sem=send.at[kind, step],
            recv_sem=recv.at[kind, step],
            device_id={"seq": to},
            device_id_type=MESH,
        )

    for kind in range(2):
        for step in range(devices):
            copy(kind, step).start()
    for kind in range(2):
        for step in range(devices):
            copy(kind, step).wait()


def pair_slots(first_ids, head_window, head_globals, head_randoms, block_count):
    count = first_ids.shape[0]
    offsets = jnp.arange(-WMAX, WMAX + 2, dtype=jnp.int32)
    named = first_ids[:, None] + offsets[None, :]
    inside = (named >= 0) & (named < block_count)
    halves = [
        inside & (jnp.abs(offsets - half)[None, :] <= head_window) for half in range(2)
    ]
    ones = jnp.ones((count, 2), bool)
    none = jnp.zeros((count, 2), bool)
    ids = jnp.concatenate(
        [
            jnp.clip(named, 0, block_count - 1),
            jnp.broadcast_to(head_globals[None, :], (count, 2)),
            head_randoms[first_ids],
            head_randoms[first_ids + 1],
        ],
        axis=1,
    )
    live = jnp.stack(
        [
            jnp.concatenate([halves[0], ones, ones, none], axis=1),
            jnp.concatenate([halves[1], ones, none, ones], axis=1),
        ],
        axis=1,
    )
    return ids, jnp.repeat(live.astype(f32), BLOCK, axis=2)


def shards(
    queries, keys, values, query_dir, key_dir, value_dir, window_width, global_blocks, random_blocks
):
    devices = lax.axis_size("seq")
    head_count = window_width.shape[0]
    group_size = devices // head_count
    device_index = lax.axis_index("seq")
    head_id = device_index // group_size
    residue = device_index % group_size
    tokens, features = queries.shape
    head_dim = features // head_count
    local_blocks = tokens // BLOCK
    own_blocks = local_blocks // group_size
    own = own_blocks * BLOCK
    block_count = local_blocks * devices
    whole = devices * tokens
    counter = 2 * jnp.arange(devices * own_blocks // 2, dtype=jnp.int32)
    first_ids = counter // own_blocks * local_blocks + residue * own_blocks + counter % own_blocks
    slots, live = pair_slots(
        first_ids,
        window_width[head_id],
        global_blocks[head_id],
        random_blocks[head_id],
        block_count,
    )
    by_block = lambda array: array.reshape(local_blocks, BLOCK, features)
    any_spec = pl.BlockSpec(memory_space=pl.ANY)
    vmem = pl.BlockSpec(memory_space=pltpu.VMEM)
    smem = pl.BlockSpec(memory_space=pltpu.SMEM)
    limit = 56 * 1024 * 1024
    count = slots.shape[0]
    shape = jax.ShapeDtypeStruct
    rows, mine = pltpu.VMEM((block_count, BLOCK, head_dim), bf16), pltpu.VMEM((devices * own, head_dim), bf16)
    dma = pltpu.SemaphoreType.DMA
    query_gn, window, fixed, drawn = pl.pallas_call(
        functools.partial(main_kernel, devices, group_size),
        out_shape=[
            shape((tokens, features), bf16),
            shape((whole + 2 * WMAX * BLOCK, 2 * head_dim), f32),
            shape((2 * BLOCK, 2 * head_dim), f32),
            shape((count * 4 * BLOCK, 2 * head_dim), bf16),
        ],
        in_specs=[smem, vmem] + [any_spec] * 6,
        out_specs=[any_spec, vmem, vmem, vmem],
        scratch_shapes=[
            mine, rows, rows, mine, rows, rows, mine,
            dma((6, devices)), dma((6, devices)), dma((devices,)), dma((devices,)),
        ],
        compiler_params=pltpu.CompilerParams(
            collective_id=0, has_side_effects=True, vmem_limit_bytes=limit
        ),
    )(
        slots, live, queries, by_block(keys), by_block(values),
        query_dir, by_block(key_dir), by_block(value_dir),
    )
    key_grad, value_grad = pl.pallas_call(
        add_kernel,
        out_shape=[shape((whole, head_dim), bf16)] * 2,
        in_specs=[smem, vmem, vmem, vmem],
        out_specs=[vmem, vmem],
        scratch_shapes=[pltpu.VMEM((whole, 2 * head_dim), f32)],
        compiler_params=pltpu.CompilerParams(vmem_limit_bytes=limit),
    )(slots, window, fixed, drawn)
    key_gn, value_gn = pl.pallas_call(
        functools.partial(return_kernel, devices, group_size),
        out_shape=[shape((group_size, tokens, features), bf16)] * 2,
        in_specs=[any_spec] * 2,
        out_specs=[any_spec] * 2,
        scratch_shapes=[dma((2, devices)), dma((2, devices))],
        compiler_params=pltpu.CompilerParams(collective_id=1, has_side_effects=True),
    )(key_grad, value_grad)

    def owner_sum(array):
        return array[0] if group_size == 1 else array.astype(f32).sum(axis=0).astype(bf16)

    return (query_gn, owner_sum(key_gn), owner_sum(value_gn))


def solution(mesh):
    rows = P(("group", "seq"), None)
    placed = (rows,) * 6 + (P("group"), P("group", None), P("group", None, None))
    return jax.shard_map(
        shards, mesh=mesh, in_specs=placed, out_specs=(rows,) * 3, check_vma=False
    )
```

```python
import functools
import math

import jax
import jax.numpy as jnp
from jax import lax
from jax.experimental import pallas as pl
from jax.experimental.pallas import tpu as pltpu
from jax.sharding import PartitionSpec as P

BLOCK = 64
WMAX = 2
PAIR = 2 * BLOCK
SLOTS = 2 * WMAX + 2 + 2 + 4
FLIGHT = 3
MESH = pl.DeviceIdType.MESH
neg_fill = -1e30
f32 = jnp.float32
bf16 = jnp.bfloat16


def dot(lhs, rhs, lhs_dim, rhs_dim):
    return lax.dot_general(
        lhs, rhs, (((lhs_dim,), (rhs_dim,)), ((), ())), preferred_element_type=f32
    )


def pair_product(qb, dqb, kg, vg, dkg, dvg, live_rows):
    head_dim = qb.shape[1]
    scale = 1.0 / math.sqrt(head_dim)
    blank = jnp.zeros((PAIR, head_dim), bf16)
    kk = jnp.concatenate([kg, dkg], axis=1)
    vv = jnp.concatenate([vg, dvg], axis=1)
    first = jnp.concatenate([qb, blank], axis=1)
    lhs = jnp.concatenate([first, jnp.concatenate([dqb, qb], axis=1)], axis=0)
    both = dot(lhs, kk, 1, 1)
    bias = jnp.concatenate(
        [jnp.broadcast_to(row, (BLOCK, SLOTS * BLOCK)) for row in live_rows], axis=0
    )
    scores = jnp.where(bias > 0.5, both[:PAIR] * scale, neg_fill)
    moved = both[PAIR:] * scale
    top = jnp.max(scores, axis=1, keepdims=True)
    weights = jnp.exp(scores - top)
    weights = weights * (1.0 / jnp.sum(weights, axis=1, keepdims=True))
    mean = jnp.sum(weights * moved, axis=1, keepdims=True)
    wb = weights.astype(bf16)
    weights_dot = (weights * (moved - mean)).astype(bf16)
    out = dot(jnp.concatenate([wb, weights_dot], axis=0), vv, 1, 0)
    tangent = (out[:PAIR, head_dim:] + out[PAIR:, :head_dim]).astype(bf16)
    pulled = dot(tangent, vg, 1, 1)
    centre = jnp.sum(weights * pulled, axis=1, keepdims=True)
    ds = (weights * (pulled - centre) * scale).astype(bf16)
    query_part = dot(ds, kg, 1, 0).astype(bf16)
    rhs = jnp.concatenate([first, jnp.concatenate([blank, tangent], axis=1)], axis=0)
    return query_part, dot(jnp.concatenate([ds, wb], axis=0), rhs, 0, 0)


def pair_live(first, width, blocks):
    slot = lax.broadcasted_iota(jnp.int32, (1, SLOTS * BLOCK), 1) // BLOCK
    near = 2 * WMAX + 2
    named = first + slot - WMAX
    rows = []
    for half in range(2):
        offset = slot - WMAX - half
        window = (slot < near) & (offset <= width) & (offset >= -width)
        window = window & (named >= 0) & (named < blocks)
        own = near + 2 + 2 * half
        other = ((slot >= near) & (slot < near + 2)) | ((slot >= own) & (slot < own + 2))
        rows.append(jnp.where(window | other, 1.0, 0.0).astype(f32))
    return rows


def greet(me, devices):
    barrier = pltpu.get_barrier_semaphore()
    for step in range(1, devices):
        pl.semaphore_signal(
            barrier, inc=1, device_id={"seq": lax.rem(me + step, devices)}, device_id_type=MESH
        )
    pl.semaphore_wait(barrier, devices - 1)


def partner(me, step, devices):
    other, place = 0, 1
    while place < devices:
        other += lax.rem(me // place + step // place, 2) * place
        place *= 2
    return other


def columns(head, head_dim):
    return pl.ds(pl.multiple_of(head * head_dim, head_dim), head_dim)


def rows_at(index, count):
    return pl.ds(pl.multiple_of(index * count, count), count)


def main_kernel(
    devices, group_size,
    widths, globals_, randoms, q, k, v, dq, dk, dv,
    q_gn, window, fixed, drawn,
    q_all, k_all, v_all, dq_all, dk_all, dv_all, q_res,
    send, recv, q_send, q_recv,
):
    me = lax.axis_index("seq")
    local_blocks = k.shape[0]
    tokens = local_blocks * BLOCK
    head_dim = k_all.shape[2]
    own = tokens // group_size
    pairs = own // PAIR
    blocks = local_blocks * devices
    head, residue = me // group_size, lax.rem(me, group_size)
    kinds = [(k, k_all), (dk, dk_all), (v, v_all), (dv, dv_all), (q, q_all), (dq, dq_all)]
    greet(me, devices)

    def copy(kind, step):
        source, target = kinds[kind]
        to = me if isinstance(step, int) and step == 0 else partner(me, step, devices)
        if kind < 4:
            part = source.at[:, :, columns(to // group_size, head_dim)]
            spot = target.at[rows_at(me, local_blocks)]
        else:
            part = source.at[
                rows_at(lax.rem(to, group_size), own), columns(to // group_size, head_dim)
            ]
            spot = target.at[rows_at(me, own), :]
        if isinstance(step, int) and step == 0:
            return pltpu.make_async_copy(part, spot, recv.at[kind, 0])
        return pltpu.make_async_remote_copy(
            src_ref=part,
            dst_ref=spot,
            send_sem=send.at[kind, step],
            recv_sem=recv.at[kind, step],
            device_id={"seq": to},
            device_id_type=MESH,
        )

    half = devices // 2
    order = list(range(half, devices)) + list(range(half))
    for kind in range(4):
        for step in order:
            copy(kind, step).start()
    for kind in (4, 5):
        for step in range(half):
            copy(kind, step).start()
    window[...] = jnp.zeros_like(window)
    fixed[...] = jnp.zeros_like(fixed)
    for step in range(half, devices):
        copy(3, step).wait_send()
        if step < half + FLIGHT:
            for kind in (4, 5):
                copy(kind, step).start()

    def send_far(place):
        @pl.when(place < half)
        def _():
            for kind in (4, 5):
                copy(kind, half + place - FLIGHT).wait_send()
                copy(kind, half + place).start()

    for kind in range(4):
        for step in range(devices):
            if step == 0:
                copy(kind, step).wait()
            else:
                copy(kind, step).wait_recv()

    def gather(ref, ids):
        return jnp.concatenate([ref[i] for i in ids], axis=0)

    def back(step, origin):
        part = q_res.at[rows_at(origin, own), :]
        target = q_gn.at[rows_at(residue, own), columns(head, head_dim)]
        return pltpu.make_async_remote_copy(
            src_ref=part,
            dst_ref=target,
            send_sem=q_send.at[step],
            recv_sem=q_recv.at[step],
            device_id={"seq": origin},
            device_id_type=MESH,
        )

    def work(step):
        origin = partner(me, step, devices)
        for pair in range(pairs):
            index = origin * pairs + pair
            rows = rows_at(index, PAIR)
            first = origin * local_blocks + residue * (own // BLOCK) + 2 * pair
            ids = [jnp.clip(first + o, 0, blocks - 1) for o in range(-WMAX, WMAX + 2)]
            ids += [globals_[2 * head + s] for s in range(2)]
            ids += [randoms[2 * (head * blocks + first) + s] for s in range(4)]
            query_part, added = pair_product(
                q_all[rows, :], dq_all[rows, :],
                gather(k_all, ids), gather(v_all, ids),
                gather(dk_all, ids), gather(dv_all, ids),
                pair_live(first, widths[head], blocks),
            )
            q_res[rows, :] = query_part
            near = (2 * WMAX + 2) * BLOCK
            spot = pl.ds(pl.multiple_of(first * BLOCK, BLOCK), near)
            window[spot, :] += added[:near]
            fixed[...] += added[near : near + PAIR]
            drawn[rows_at(index, 2 * PAIR), :] = added[near + PAIR :].astype(bf16)
        return origin

    own_copy = pltpu.make_async_copy(
        q_res.at[rows_at(me, own), :],
        q_gn.at[rows_at(residue, own), columns(head, head_dim)],
        q_recv.at[0],
    )
    copy(4, 0).wait()
    copy(5, 0).wait()

    def wait_rows(step):
        origin = partner(me, step, devices)
        for kind in (4, 5):
            source, target = kinds[kind]
            pltpu.make_async_remote_copy(
                src_ref=source.at[rows_at(residue, own), columns(head, head_dim)],
                dst_ref=target.at[rows_at(origin, own), :],
                send_sem=send.at[kind, step],
                recv_sem=recv.at[kind, step],
                device_id={"seq": origin},
                device_id_type=MESH,
            ).wait_recv()

    @pl.loop(0, half)
    def _(step):
        @pl.when(step > 0)
        def _():
            wait_rows(step)

        origin = work(step)

        @pl.when(step > 0)
        def _():
            back(step, origin).start()

        @pl.when(step == 0)
        def _():
            own_copy.start()

        @pl.when(lax.rem(step, 2) == 1)
        def _():
            send_far(FLIGHT + step // 2)

    @pl.loop(half, devices)
    def _(step):
        send_far(FLIGHT + half // 2 + step - half)
        wait_rows(step)
        back(step, work(step)).start()

    for kind in range(6):
        for step in range(1, devices):
            if step < half or kind in (0, 1, 2) or (kind > 3 and step >= devices - FLIGHT):
                copy(kind, step).wait_send()
    own_copy.wait()
    for step in range(1, devices):
        giver = partner(me, step, devices)
        pltpu.make_async_remote_copy(
            src_ref=q_res.at[rows_at(giver, own), :],
            dst_ref=q_gn.at[
                rows_at(lax.rem(giver, group_size), own),
                columns(giver // group_size, head_dim),
            ],
            send_sem=q_send.at[step],
            recv_sem=q_recv.at[step],
            device_id={"seq": giver},
            device_id_type=MESH,
        ).wait()


def add_kernel(group_size, local_blocks, globals_, randoms, window, fixed, drawn, k_out, v_out, acc):
    tokens, head_dim = k_out.shape
    blocks = tokens // BLOCK
    me = lax.axis_index("seq")
    head, residue = me // group_size, lax.rem(me, group_size)
    own_blocks = local_blocks // group_size
    pairs = own_blocks // 2
    acc[...] = window[pl.ds(WMAX * BLOCK, tokens), :]
    for s in range(2):
        rows = rows_at(globals_[2 * head + s], BLOCK)
        acc[rows, :] += fixed[s * BLOCK : (s + 1) * BLOCK, :]

    @pl.loop(0, drawn.shape[0] // (4 * BLOCK))
    def _(index):
        first = index // pairs * local_blocks + residue * own_blocks + 2 * lax.rem(index, pairs)
        for s in range(4):
            rows = rows_at(randoms[2 * (head * blocks + first) + s], BLOCK)
            acc[rows, :] += drawn[rows_at(index * 4 + s, BLOCK), :].astype(f32)

    k_out[...] = acc[:, :head_dim].astype(bf16)
    v_out[...] = acc[:, head_dim:].astype(bf16)


def return_kernel(devices, group_size, k, v, k_gn, v_gn, send, recv):
    me = lax.axis_index("seq")
    tokens, head_dim = k.shape[0] // devices, k.shape[1]
    greet(me, devices)

    def copy(kind, step):
        source, target = ((k, k_gn), (v, v_gn))[kind]
        to = partner(me, step, devices)
        part = source.at[rows_at(to, tokens), :]
        spot = target.at[lax.rem(me, group_size), :, columns(me // group_size, head_dim)]
        if isinstance(step, int) and step == 0:
            return pltpu.make_async_copy(part, spot, recv.at[kind, 0])
        return pltpu.make_async_remote_copy(
            src_ref=part,
            dst_ref=spot,
            send_sem=send.at[kind, step],
            recv_sem=recv.at[kind, step],
            device_id={"seq": to},
            device_id_type=MESH,
        )

    half = devices // 2
    for step in list(range(half, devices)) + list(range(half)):
        for kind in range(2):
            copy(kind, step).start()
    for kind in range(2):
        for step in range(devices):
            copy(kind, step).wait()


def shards(
    queries, keys, values, query_dir, key_dir, value_dir, window_width, global_blocks, random_blocks
):
    devices = lax.axis_size("seq")
    head_count = window_width.shape[0]
    group_size = devices // head_count
    tokens, features = queries.shape
    head_dim = features // head_count
    local_blocks = tokens // BLOCK
    own_blocks = local_blocks // group_size
    own = own_blocks * BLOCK
    block_count = local_blocks * devices
    whole = devices * tokens
    by_block = lambda array: array.reshape(local_blocks, BLOCK, features)
    any_spec = pl.BlockSpec(memory_space=pl.ANY)
    vmem = pl.BlockSpec(memory_space=pltpu.VMEM)
    smem = pl.BlockSpec(memory_space=pltpu.SMEM)
    limit = 56 * 1024 * 1024
    count = devices * own_blocks // 2
    named = (global_blocks.reshape(-1), random_blocks.reshape(-1))
    shape = jax.ShapeDtypeStruct
    rows, mine = pltpu.VMEM((block_count, BLOCK, head_dim), bf16), pltpu.VMEM((devices * own, head_dim), bf16)
    dma = pltpu.SemaphoreType.DMA
    query_gn, window, fixed, drawn = pl.pallas_call(
        functools.partial(main_kernel, devices, group_size),
        out_shape=[
            shape((tokens, features), bf16),
            shape((whole + 2 * WMAX * BLOCK, 2 * head_dim), f32),
            shape((2 * BLOCK, 2 * head_dim), f32),
            shape((count * 4 * BLOCK, 2 * head_dim), bf16),
        ],
        in_specs=[smem] * 3 + [any_spec] * 6,
        out_specs=[any_spec, vmem, vmem, vmem],
        scratch_shapes=[
            mine, rows, rows, mine, rows, rows, mine,
            dma((6, devices)), dma((6, devices)), dma((devices,)), dma((devices,)),
        ],
        compiler_params=pltpu.CompilerParams(
            collective_id=0, has_side_effects=True, vmem_limit_bytes=limit
        ),
    )(
        window_width, *named, queries, by_block(keys), by_block(values),
        query_dir, by_block(key_dir), by_block(value_dir),
    )
    key_grad, value_grad = pl.pallas_call(
        functools.partial(add_kernel, group_size, local_blocks),
        out_shape=[shape((whole, head_dim), bf16)] * 2,
        in_specs=[smem, smem, vmem, vmem, vmem],
        out_specs=[vmem, vmem],
        scratch_shapes=[pltpu.VMEM((whole, 2 * head_dim), f32)],
        compiler_params=pltpu.CompilerParams(vmem_limit_bytes=limit),
    )(*named, window, fixed, drawn)
    key_gn, value_gn = pl.pallas_call(
        functools.partial(return_kernel, devices, group_size),
        out_shape=[shape((group_size, tokens, features), bf16)] * 2,
        in_specs=[any_spec] * 2,
        out_specs=[any_spec] * 2,
        scratch_shapes=[dma((2, devices)), dma((2, devices))],
        compiler_params=pltpu.CompilerParams(collective_id=1, has_side_effects=True),
    )(key_grad, value_grad)

    def owner_sum(array):
        return array[0] if group_size == 1 else array.astype(f32).sum(axis=0).astype(bf16)

    return (query_gn, owner_sum(key_gn), owner_sum(value_gn))


def solution(mesh):
    rows = P(("group", "seq"), None)
    placed = (rows,) * 6 + (P("group"), P("group", None), P("group", None, None))
    return jax.shard_map(
        shards, mesh=mesh, in_specs=placed, out_specs=(rows,) * 3, check_vma=False
    )
```

```python
import functools
import math

import jax
import jax.numpy as jnp
from jax import lax
from jax.experimental import pallas as pl
from jax.experimental.pallas import tpu as pltpu
from jax.sharding import PartitionSpec as P

BLOCK = 64
WMAX = 2
PAIR = 2 * BLOCK
SLOTS = 2 * WMAX + 2 + 2 + 4
FLIGHT = 3
MESH = pl.DeviceIdType.MESH
neg_fill = -1e30
f32 = jnp.float32
bf16 = jnp.bfloat16


def dot(lhs, rhs, lhs_dim, rhs_dim):
    return lax.dot_general(
        lhs, rhs, (((lhs_dim,), (rhs_dim,)), ((), ())), preferred_element_type=f32
    )


def pair_product(qb, dqb, kg, vg, dkg, dvg, live_rows):
    head_dim = qb.shape[1]
    scale = 1.0 / math.sqrt(head_dim)
    blank = jnp.zeros((PAIR, head_dim), bf16)
    kk = jnp.concatenate([kg, dkg], axis=1)
    vv = jnp.concatenate([vg, dvg], axis=1)
    first = jnp.concatenate([qb, blank], axis=1)
    lhs = jnp.concatenate([first, jnp.concatenate([dqb, qb], axis=1)], axis=0)
    both = dot(lhs, kk, 1, 1)
    bias = jnp.concatenate(
        [jnp.broadcast_to(row, (BLOCK, SLOTS * BLOCK)) for row in live_rows], axis=0
    )
    scores = jnp.where(bias > 0.5, both[:PAIR] * scale, neg_fill)
    moved = both[PAIR:] * scale
    top = jnp.max(scores, axis=1, keepdims=True)
    weights = jnp.exp(scores - top)
    weights = weights * (1.0 / jnp.sum(weights, axis=1, keepdims=True))
    mean = jnp.sum(weights * moved, axis=1, keepdims=True)
    wb = weights.astype(bf16)
    weights_dot = (weights * (moved - mean)).astype(bf16)
    out = dot(jnp.concatenate([wb, weights_dot], axis=0), vv, 1, 0)
    tangent = (out[:PAIR, head_dim:] + out[PAIR:, :head_dim]).astype(bf16)
    pulled = dot(tangent, vg, 1, 1)
    centre = jnp.sum(weights * pulled, axis=1, keepdims=True)
    ds = (weights * (pulled - centre) * scale).astype(bf16)
    query_part = dot(ds, kg, 1, 0).astype(bf16)
    rhs = jnp.concatenate([first, jnp.concatenate([blank, tangent], axis=1)], axis=0)
    return query_part, dot(jnp.concatenate([ds, wb], axis=0), rhs, 0, 0)


def pair_live(first, width, blocks):
    slot = lax.broadcasted_iota(jnp.int32, (1, SLOTS * BLOCK), 1) // BLOCK
    near = 2 * WMAX + 2
    named = first + slot - WMAX
    rows = []
    for half in range(2):
        offset = slot - WMAX - half
        window = (slot < near) & (offset <= width) & (offset >= -width)
        window = window & (named >= 0) & (named < blocks)
        own = near + 2 + 2 * half
        other = ((slot >= near) & (slot < near + 2)) | ((slot >= own) & (slot < own + 2))
        rows.append(jnp.where(window | other, 1.0, 0.0).astype(f32))
    return rows


def greet(me, devices):
    barrier = pltpu.get_barrier_semaphore()
    for step in range(1, devices):
        pl.semaphore_signal(
            barrier, inc=1, device_id={"seq": lax.rem(me + step, devices)}, device_id_type=MESH
        )
    pl.semaphore_wait(barrier, devices - 1)


def partner(me, step, devices):
    other, place = 0, 1
    while place < devices:
        other += lax.rem(me // place + step // place, 2) * place
        place *= 2
    return other


def columns(head, head_dim):
    return pl.ds(pl.multiple_of(head * head_dim, head_dim), head_dim)


def rows_at(index, count):
    return pl.ds(pl.multiple_of(index * count, count), count)


def main_kernel(
    devices, group_size,
    widths, globals_, randoms, q, k, v, dq, dk, dv,
    q_gn, window, fixed, drawn,
    q_all, k_all, v_all, dq_all, dk_all, dv_all, q_res,
    send, recv, q_send, q_recv,
):
    me = lax.axis_index("seq")
    local_blocks = k.shape[0]
    tokens = local_blocks * BLOCK
    head_dim = k_all.shape[2]
    own = tokens // group_size
    pairs = own // PAIR
    blocks = local_blocks * devices
    head, residue = me // group_size, lax.rem(me, group_size)
    kinds = [(k, k_all), (dk, dk_all), (v, v_all), (dv, dv_all), (q, q_all), (dq, dq_all)]
    greet(me, devices)

    def copy(kind, step):
        source, target = kinds[kind]
        to = me if isinstance(step, int) and step == 0 else partner(me, step, devices)
        if kind < 4:
            part = source.at[:, :, columns(to // group_size, head_dim)]
            spot = target.at[rows_at(me, local_blocks)]
        else:
            part = source.at[
                rows_at(lax.rem(to, group_size), own), columns(to // group_size, head_dim)
            ]
            spot = target.at[rows_at(me, own), :]
        if isinstance(step, int) and step == 0:
            return pltpu.make_async_copy(part, spot, recv.at[kind, 0])
        return pltpu.make_async_remote_copy(
            src_ref=part,
            dst_ref=spot,
            send_sem=send.at[kind, step],
            recv_sem=recv.at[kind, step],
            device_id={"seq": to},
            device_id_type=MESH,
        )

    half = devices // 2
    order = [step for near in range(half) for step in (half + near, near)]
    for kind in range(4):
        for step in order:
            copy(kind, step).start()
    for kind in (4, 5):
        for step in range(half):
            copy(kind, step).start()
    window[...] = jnp.zeros_like(window)
    fixed[...] = jnp.zeros_like(fixed)
    for step in range(half, devices):
        copy(3, step).wait_send()
        if step < half + FLIGHT:
            for kind in (4, 5):
                copy(kind, step).start()

    def send_far(place):
        @pl.when(place < half)
        def _():
            for kind in (4, 5):
                copy(kind, half + place - FLIGHT).wait_send()
                copy(kind, half + place).start()

    for kind in range(4):
        for step in range(devices):
            if step == 0:
                copy(kind, step).wait()
            else:
                copy(kind, step).wait_recv()

    def gather(ref, ids):
        return jnp.concatenate([ref[i] for i in ids], axis=0)

    def back(step, origin):
        part = q_res.at[rows_at(origin, own), :]
        target = q_gn.at[rows_at(residue, own), columns(head, head_dim)]
        return pltpu.make_async_remote_copy(
            src_ref=part,
            dst_ref=target,
            send_sem=q_send.at[step],
            recv_sem=q_recv.at[step],
            device_id={"seq": origin},
            device_id_type=MESH,
        )

    def work(step):
        origin = partner(me, step, devices)
        for pair in range(pairs):
            index = origin * pairs + pair
            rows = rows_at(index, PAIR)
            first = origin * local_blocks + residue * (own // BLOCK) + 2 * pair
            ids = [jnp.clip(first + o, 0, blocks - 1) for o in range(-WMAX, WMAX + 2)]
            ids += [globals_[2 * head + s] for s in range(2)]
            ids += [randoms[2 * (head * blocks + first) + s] for s in range(4)]
            query_part, added = pair_product(
                q_all[rows, :], dq_all[rows, :],
                gather(k_all, ids), gather(v_all, ids),
                gather(dk_all, ids), gather(dv_all, ids),
                pair_live(first, widths[head], blocks),
            )
            q_res[rows, :] = query_part
            near = (2 * WMAX + 2) * BLOCK
            spot = pl.ds(pl.multiple_of(first * BLOCK, BLOCK), near)
            window[spot, :] += added[:near]
            fixed[...] += added[near : near + PAIR]
            drawn[rows_at(index, 2 * PAIR), :] = added[near + PAIR :].astype(bf16)
        return origin

    own_copy = pltpu.make_async_copy(
        q_res.at[rows_at(me, own), :],
        q_gn.at[rows_at(residue, own), columns(head, head_dim)],
        q_recv.at[0],
    )
    copy(4, 0).wait()
    copy(5, 0).wait()

    def wait_rows(step):
        origin = partner(me, step, devices)
        for kind in (4, 5):
            source, target = kinds[kind]
            pltpu.make_async_remote_copy(
                src_ref=source.at[rows_at(residue, own), columns(head, head_dim)],
                dst_ref=target.at[rows_at(origin, own), :],
                send_sem=send.at[kind, step],
                recv_sem=recv.at[kind, step],
                device_id={"seq": origin},
                device_id_type=MESH,
            ).wait_recv()

    @pl.loop(0, half)
    def _(step):
        @pl.when(step > 0)
        def _():
            wait_rows(step)

        origin = work(step)

        @pl.when(step > 0)
        def _():
            back(step, origin).start()

        @pl.when(step == 0)
        def _():
            own_copy.start()

        @pl.when(lax.rem(step, 2) == 1)
        def _():
            send_far(FLIGHT + step // 2)

    @pl.loop(half, devices)
    def _(step):
        send_far(FLIGHT + half // 2 + step - half)
        wait_rows(step)
        back(step, work(step)).start()

    for kind in range(6):
        for step in range(1, devices):
            if step < half or kind in (0, 1, 2) or (kind > 3 and step >= devices - FLIGHT):
                copy(kind, step).wait_send()
    own_copy.wait()
    for step in range(1, devices):
        giver = partner(me, step, devices)
        pltpu.make_async_remote_copy(
            src_ref=q_res.at[rows_at(giver, own), :],
            dst_ref=q_gn.at[
                rows_at(lax.rem(giver, group_size), own),
                columns(giver // group_size, head_dim),
            ],
            send_sem=q_send.at[step],
            recv_sem=q_recv.at[step],
            device_id={"seq": giver},
            device_id_type=MESH,
        ).wait()


def add_kernel(group_size, local_blocks, globals_, randoms, window, fixed, drawn, k_out, v_out, acc):
    tokens, head_dim = k_out.shape
    blocks = tokens // BLOCK
    me = lax.axis_index("seq")
    head, residue = me // group_size, lax.rem(me, group_size)
    own_blocks = local_blocks // group_size
    pairs = own_blocks // 2
    acc[...] = window[pl.ds(WMAX * BLOCK, tokens), :]
    for s in range(2):
        rows = rows_at(globals_[2 * head + s], BLOCK)
        acc[rows, :] += fixed[s * BLOCK : (s + 1) * BLOCK, :]

    @pl.loop(0, drawn.shape[0] // (4 * BLOCK))
    def _(index):
        first = index // pairs * local_blocks + residue * own_blocks + 2 * lax.rem(index, pairs)
        for s in range(4):
            rows = rows_at(randoms[2 * (head * blocks + first) + s], BLOCK)
            acc[rows, :] += drawn[rows_at(index * 4 + s, BLOCK), :].astype(f32)

    k_out[...] = acc[:, :head_dim].astype(bf16)
    v_out[...] = acc[:, head_dim:].astype(bf16)


def return_kernel(devices, group_size, k, v, k_gn, v_gn, send, recv):
    me = lax.axis_index("seq")
    tokens, head_dim = k.shape[0] // devices, k.shape[1]
    greet(me, devices)

    def copy(kind, step):
        source, target = ((k, k_gn), (v, v_gn))[kind]
        to = partner(me, step, devices)
        part = source.at[rows_at(to, tokens), :]
        spot = target.at[lax.rem(me, group_size), :, columns(me // group_size, head_dim)]
        if isinstance(step, int) and step == 0:
            return pltpu.make_async_copy(part, spot, recv.at[kind, 0])
        return pltpu.make_async_remote_copy(
            src_ref=part,
            dst_ref=spot,
            send_sem=send.at[kind, step],
            recv_sem=recv.at[kind, step],
            device_id={"seq": to},
            device_id_type=MESH,
        )

    half = devices // 2
    for step in [step for near in range(half) for step in (half + near, near)]:
        for kind in range(2):
            copy(kind, step).start()
    for kind in range(2):
        for step in range(devices):
            copy(kind, step).wait()


def shards(
    queries, keys, values, query_dir, key_dir, value_dir, window_width, global_blocks, random_blocks
):
    devices = lax.axis_size("seq")
    head_count = window_width.shape[0]
    group_size = devices // head_count
    tokens, features = queries.shape
    head_dim = features // head_count
    local_blocks = tokens // BLOCK
    own_blocks = local_blocks // group_size
    own = own_blocks * BLOCK
    block_count = local_blocks * devices
    whole = devices * tokens
    by_block = lambda array: array.reshape(local_blocks, BLOCK, features)
    any_spec = pl.BlockSpec(memory_space=pl.ANY)
    vmem = pl.BlockSpec(memory_space=pltpu.VMEM)
    smem = pl.BlockSpec(memory_space=pltpu.SMEM)
    limit = 56 * 1024 * 1024
    count = devices * own_blocks // 2
    named = (global_blocks.reshape(-1), random_blocks.reshape(-1))
    shape = jax.ShapeDtypeStruct
    rows, mine = pltpu.VMEM((block_count, BLOCK, head_dim), bf16), pltpu.VMEM((devices * own, head_dim), bf16)
    dma = pltpu.SemaphoreType.DMA
    query_gn, window, fixed, drawn = pl.pallas_call(
        functools.partial(main_kernel, devices, group_size),
        out_shape=[
            shape((tokens, features), bf16),
            shape((whole + 2 * WMAX * BLOCK, 2 * head_dim), f32),
            shape((2 * BLOCK, 2 * head_dim), f32),
            shape((count * 4 * BLOCK, 2 * head_dim), bf16),
        ],
        in_specs=[smem] * 3 + [any_spec] * 6,
        out_specs=[any_spec, vmem, vmem, vmem],
        scratch_shapes=[
            mine, rows, rows, mine, rows, rows, mine,
            dma((6, devices)), dma((6, devices)), dma((devices,)), dma((devices,)),
        ],
        compiler_params=pltpu.CompilerParams(
            collective_id=0, has_side_effects=True, vmem_limit_bytes=limit
        ),
    )(
        window_width, *named, queries, by_block(keys), by_block(values),
        query_dir, by_block(key_dir), by_block(value_dir),
    )
    key_grad, value_grad = pl.pallas_call(
        functools.partial(add_kernel, group_size, local_blocks),
        out_shape=[shape((whole, head_dim), bf16)] * 2,
        in_specs=[smem, smem, vmem, vmem, vmem],
        out_specs=[vmem, vmem],
        scratch_shapes=[pltpu.VMEM((whole, 2 * head_dim), f32)],
        compiler_params=pltpu.CompilerParams(vmem_limit_bytes=limit),
    )(*named, window, fixed, drawn)
    key_gn, value_gn = pl.pallas_call(
        functools.partial(return_kernel, devices, group_size),
        out_shape=[shape((group_size, tokens, features), bf16)] * 2,
        in_specs=[any_spec] * 2,
        out_specs=[any_spec] * 2,
        scratch_shapes=[dma((2, devices)), dma((2, devices))],
        compiler_params=pltpu.CompilerParams(collective_id=1, has_side_effects=True),
    )(key_grad, value_grad)

    def owner_sum(array):
        return array[0] if group_size == 1 else array.astype(f32).sum(axis=0).astype(bf16)

    return (query_gn, owner_sum(key_gn), owner_sum(value_gn))


def solution(mesh):
    rows = P(("group", "seq"), None)
    placed = (rows,) * 6 + (P("group"), P("group", None), P("group", None, None))
    return jax.shard_map(
        shards, mesh=mesh, in_specs=placed, out_specs=(rows,) * 3, check_vma=False
    )
```
